512 devices in a mesh: tm: 32 (over x, y), space: 16 (over z, core).
Axes of the slice: x: 4, y: 8, z: 8, core: 2. Of those that a mesh axis runs over, the one named last changes fastest.
Arguments:
- frames: bfloat16 [64, 16, 16, 32, 256], P('tm', 'space'), may hold values from -60 to 60
- norm_gain: float32 [256], replicated, may hold values from 0.1 to 1.9
- norm_shift: float32 [256], replicated, may hold values from -3 to 3
- conv_filter: bfloat16 [3, 3, 3, 256, 256], replicated, may hold values from -0.078125 to 0.078125
- conv_offset: float32 [256], replicated, may hold values from -3 to 3
Outputs:
- block_out: bfloat16 [64, 16, 16, 32, 256], P('tm', 'space')
The draws below stay inside these ranges and needn't reach their ends.
All inputs are finite; a program needn't handle non-finite values.
Results may differ from the reference program's by a relative error of at most 0.0015.
The reference program's roundings to bfloat16 on the way (of `act`) count: a program that leaves them out, or rounds other values in their place, can miss the bound.
Values may be sent and summed in bfloat16 or wider, within the bound.
No kernel may reach another device: no remote copies, remote signals or barrier semaphores. Data moves between devices by JAX's collectives and lax.ppermute only.
A program may use at most 64 MiB of HBM per device.

```python
import math
import jax
import jax.numpy as jnp
from jax import lax

C = 256
GROUPS = 32
TH = 16
TW = 32
TIMES = 64
TILES = 16
GRID_X = 4
GRID_Y = 4


def draw_frames(key, part):
    key = jax.random.fold_in(key, 11)
    keys = jax.random.split(key, 4)
    moments = jnp.arange(TIMES, dtype=jnp.float32)
    ramp = 0.5 * jnp.power(3.0, moments / max(TIMES - 1, 1))
    jitter = jax.random.uniform(keys[0], (TIMES,), jnp.float32, 0.8, 1.25)
    channel_scale = jnp.exp(jax.random.uniform(keys[1], (C,), jnp.float32, math.log(0.3), math.log(3.0)))
    shape = (TIMES, TILES, TH, TW, C)
    channel_mean = jnp.clip(0.6 * jax.random.normal(keys[2], (C,), jnp.float32), -3.0, 3.0)
    noise = jnp.clip(jax.random.normal(keys[3], shape, jnp.float32), -5.0, 5.0)
    level = (ramp * jitter)[:, None, None, None, None]
    return (level * channel_scale * (channel_mean + noise)).astype(jnp.bfloat16)


def centred(key, shape, width, most, held_as=jnp.bfloat16):
    return jnp.clip(width * jax.random.normal(key, shape, jnp.float32), -most, most).astype(held_as)


def setup_inputs(seed: int = 0) -> dict:
    arg_keys = jax.random.split(jax.random.key(seed), 6)
    return {
        "frames": draw_frames(jax.random.fold_in(arg_keys[5], 71), 0),
        "norm_gain": jnp.clip(1.0 + 0.18 * jax.random.normal(arg_keys[1], (C,), jnp.float32), 0.1, 1.9),
        "norm_shift": centred(arg_keys[2], (C,), 0.5, 3.0, jnp.float32),
        "conv_filter": centred(arg_keys[3], (3, 3, 3, C, C), (27 * C) ** -0.5, 0.078125),
        "conv_offset": centred(arg_keys[4], (C,), 0.3, 3.0, jnp.float32),
    }


def to_whole(tiled):
    shaped = tiled.reshape(TIMES, GRID_Y, GRID_X, TH, TW, C)
    return shaped.transpose(0, 1, 3, 2, 4, 5).reshape(TIMES, GRID_Y * TH, GRID_X * TW, C)

def to_tiles(whole):
    shaped = whole.reshape(TIMES, GRID_Y, TH, GRID_X, TW, C)
    return shaped.transpose(0, 1, 3, 2, 4, 5).reshape(TIMES, GRID_Y * GRID_X, TH, TW, C)

def causal_norm(values, gain, shift):
    width_group = C // GROUPS
    plain = lax.optimization_barrier(jnp.sum(values, axis=(1, 2))).reshape(TIMES, GROUPS, width_group).sum(-1)
    square = lax.optimization_barrier(jnp.sum(values * values, axis=(1, 2))).reshape(TIMES, GROUPS, width_group).sum(-1)
    run_plain = jnp.cumsum(plain, axis=0)
    run_square = jnp.cumsum(square, axis=0)
    cells = values.shape[1] * values.shape[2] * width_group
    count = (jnp.arange(TIMES, dtype=jnp.int32) + 1).astype(jnp.float32) * cells
    mean = run_plain / count[:, None]
    spread = run_square / count[:, None] - mean * mean
    inverse = lax.rsqrt(spread + 1e-06)
    mean_wide = jnp.repeat(mean, width_group, axis=1)
    inverse_wide = jnp.repeat(inverse, width_group, axis=1)
    normed = (values - mean_wide[:, None, None, :]) * inverse_wide[:, None, None, :] * gain + shift
    return jax.nn.silu(normed)

def causal_conv(active, kernel, offset):
    source = active.astype(jnp.float32)[None]
    source = jnp.pad(source, ((0, 0), (2, 0), (1, 1), (1, 1), (0, 0)))
    result = lax.conv_general_dilated(source, kernel.astype(jnp.float32), (1, 1, 1), 'VALID', dimension_numbers=('NDHWC', 'DHWIO', 'NDHWC'), precision=lax.Precision.HIGHEST)
    return result[0] + offset

def reference(frames, norm_gain, norm_shift, conv_filter, conv_offset):
    inputs = to_whole(frames).astype(jnp.float32)
    act = causal_norm(inputs, norm_gain, norm_shift).astype(jnp.bfloat16)
    output = (inputs + causal_conv(act, conv_filter, conv_offset)).astype(jnp.bfloat16)
    return to_tiles(output)
```

```python
import functools

import jax
import jax.numpy as jnp
from jax import lax
from jax.experimental import pallas as pl
from jax.experimental.pallas import tpu as pltpu
from jax.sharding import PartitionSpec as P

GROUPS = 32
ACROSS = 4
F32, BF16 = jnp.float32, jnp.bfloat16


def split(value):
    high = value.astype(BF16)
    rest = value - high.astype(F32)
    middle = rest.astype(BF16)
    low = (rest - middle.astype(F32)).astype(BF16)
    return high, middle, low


def exact_dot(value, table):
    return sum(jnp.dot(part, table, preferred_element_type=F32) for part in split(value))


def sums_kernel(frames_ref, out_ref):
    frames, height, width, channels = frames_ref.shape
    per_group = channels // GROUPS
    channel = lax.broadcasted_iota(jnp.int32, (channels, 128), 0)
    lane = lax.broadcasted_iota(jnp.int32, (channels, 128), 1)
    total = jnp.zeros((8, 128), F32)
    for frame in range(frames):
        plain = jnp.zeros((8, channels), F32)
        square = jnp.zeros((8, channels), F32)
        for row in range(height):
            block = frames_ref[frame, row].astype(F32).reshape(width // 8, 8, channels)
            plain = plain + block.sum(0)
            square = square + (block * block).sum(0)
        for kind, value in enumerate((plain, square)):
            slot = (kind * frames + frame) * GROUPS
            table = jnp.where(lane == slot + channel // per_group, 1.0, 0.0).astype(BF16)
            total = total + exact_dot(value, table)
    row = total.sum(0, keepdims=True)
    out_ref[...] = jnp.broadcast_to(row[None], out_ref.shape)


def group_sums(frames, peers):
    return pl.pallas_call(
        sums_kernel,
        out_shape=jax.ShapeDtypeStruct((peers, 1, 128), F32),
        in_specs=[pl.BlockSpec(memory_space=pltpu.VMEM)],
        out_specs=pl.BlockSpec(memory_space=pltpu.VMEM),
        cost_estimate=pl.CostEstimate(flops=1 << 20, bytes_accessed=1 << 19, transcendentals=0),
    )(frames)


def conv_kernel(place_ref, sums_ref, own_ref, past_ref, edge_ref, past_edge_ref, gain_ref, shift_ref, filter_ref,
                offset_ref, out_ref, shifted):
    frames, height, width, channels = own_ref.shape
    per_group = channels // GROUPS
    time, tile = place_ref[0], place_ref[1]
    tiles = place_ref[2]
    row_of, col_of = tile // ACROSS, tile % ACROSS
    down_max = tiles // ACROSS - 1

    sums = sums_ref[...]
    index = lax.broadcasted_iota(jnp.int32, sums.shape, 0)
    lane = lax.broadcasted_iota(jnp.int32, (1, 128), 1)
    first = jnp.where((lane // GROUPS) % 2 == 0, 1.0, 0.0).astype(F32)
    before = jnp.where(index < time - 1, sums, 0.0).sum(0, keepdims=True)
    past = jnp.where(index == time - 1, sums, 0.0).sum(0, keepdims=True)
    own = jnp.where(index == time, sums, 0.0).sum(0, keepdims=True)
    running = jnp.concatenate(
        [before + past * first, before + past, before + past + own * first, before + past + own]
        + [jnp.zeros((4, 128), F32)],
        axis=0,
    )
    slot = lax.broadcasted_iota(jnp.int32, (128, channels), 0)
    channel = lax.broadcasted_iota(jnp.int32, (128, channels), 1)
    wide = []
    for kind in range(2):
        table = (slot // (2 * GROUPS) == kind) & (slot % GROUPS == channel // per_group)
        wide.append(exact_dot(running, jnp.where(table, 1.0, 0.0).astype(BF16)))
    frame_row = lax.broadcasted_iota(jnp.int32, (8, channels), 0)
    cells = height * width * tiles * per_group
    count = jnp.maximum((time * 2 - 1 + frame_row) * cells, 1).astype(F32)
    mean = wide[0] / count
    spread = wide[1] / count - mean * mean
    scale = lax.rsqrt(spread + 1e-06) * gain_ref[...]
    shift = shift_ref[...]

    def activate(value, which):
        u = (value.astype(F32) - mean[which : which + 1]) * scale[which : which + 1] + shift
        return u / (1.0 + jnp.exp(-u))

    has_left = jnp.where(col_of > 0, 1.0, 0.0).astype(F32)
    has_right = jnp.where(col_of < ACROSS - 1, 1.0, 0.0).astype(F32)
    has_up = jnp.where(row_of > 0, 1.0, 0.0).astype(F32)
    has_down = jnp.where(row_of < down_max, 1.0, 0.0).astype(F32)
    has_past = jnp.where(time > 0, 1.0, 0.0).astype(F32)
    up_at = 2 * height
    down_at = up_at + width
    corner_at = down_at + width

    def put(which, row, center, left, right):
        at = pl.ds((which * (height + 2) + row) * width, width)
        place = lax.broadcasted_iota(jnp.int32, (width, channels), 0)
        toward = jnp.where(place == 0, left, pltpu.roll(center, 1, 0))
        away = jnp.where(place == width - 1, right, pltpu.roll(center, width - 1, 0))
        shifted[at, 0:channels] = toward.astype(BF16)
        shifted[at, channels : 2 * channels] = center.astype(BF16)
        shifted[at, 2 * channels : 3 * channels] = away.astype(BF16)

    for which in range(4):
        source = past_ref if which < 2 else own_ref
        edges = past_edge_ref if which < 2 else edge_ref
        here = has_past if which < 2 else jnp.ones((), F32)
        frame = which % 2
        left = activate(edges[frame, 0:height], which) * (has_left * here)
        right = activate(edges[frame, height : 2 * height], which) * (has_right * here)
        up = activate(edges[frame, up_at:down_at], which) * (has_up * here)
        down = activate(edges[frame, down_at:corner_at], which) * (has_down * here)
        corners = activate(edges[frame, corner_at : corner_at + 16], which) * here
        put(which, 0, up, corners[0:1] * (has_up * has_left), corners[1:2] * (has_up * has_right))
        put(which, height + 1, down, corners[2:3] * (has_down * has_left), corners[3:4] * (has_down * has_right))
        for row in range(height):
            center = activate(source[frame, row], which) * here
            put(which, row + 1, center, left[row : row + 1], right[row : row + 1])

    for frame in range(frames):
        total = jnp.zeros((height * width, channels), F32)
        for lagged in range(3):
            for vertical in range(3):
                at = ((frame + lagged) * (height + 2) + vertical) * width
                total = total + jnp.dot(
                    shifted[at : at + height * width, :],
                    filter_ref[lagged * 3 + vertical],
                    preferred_element_type=F32,
                )
        value = own_ref[frame].astype(F32).reshape(height * width, channels)
        value = value + (total + offset_ref[...])
        out_ref[frame] = value.astype(BF16).reshape(height, width, channels)


def convolve(place, sums, own, past, edge, past_edge, gain, shift, taps, offset):
    frames, height, width, channels = own.shape
    vmem = pl.BlockSpec(memory_space=pltpu.VMEM)
    return pl.pallas_call(
        conv_kernel,
        out_shape=jax.ShapeDtypeStruct(own.shape, BF16),
        in_specs=[pl.BlockSpec(memory_space=pltpu.SMEM)] + [vmem] * 9,
        out_specs=vmem,
        scratch_shapes=[
            pltpu.VMEM((4 * (height + 2) * width, 3 * channels), BF16),
        ],
        compiler_params=pltpu.CompilerParams(vmem_limit_bytes=40 << 20),
        cost_estimate=pl.CostEstimate(flops=4 << 30, bytes_accessed=6 << 20, transcendentals=1 << 20),
    )(place, sums, own, past, edge, past_edge, gain, shift, taps, offset)


def local(frames, norm_gain, norm_shift, conv_filter, conv_offset):
    own = frames[:, 0]
    count, height, width, channels = own.shape
    times, tiles = lax.axis_size("tm"), lax.axis_size("space")
    place = jnp.stack([lax.axis_index("tm"), lax.axis_index("space"), jnp.int32(tiles)]).astype(jnp.int32)

    later = [(t, t + 1) for t in range(times - 1)]
    rightward = [(s, s + 1) for s in range(tiles) if s % ACROSS < ACROSS - 1]
    leftward = [(s, s - 1) for s in range(tiles) if s % ACROSS > 0]
    downward = [(s, s + ACROSS) for s in range(tiles - ACROSS)]
    upward = [(s, s - ACROSS) for s in range(ACROSS, tiles)]

    sums = group_sums(own, tiles)
    past = lax.ppermute(own, "tm", later)
    left = lax.ppermute(own[:, :, -1], "space", rightward)
    right = lax.ppermute(own[:, :, 0], "space", leftward)
    sums = lax.all_to_all(sums, "space", 0, 0).sum(0, keepdims=True)
    last = jnp.concatenate([own[:, -1], left[:, -1:], right[:, -1:]], axis=1)
    start = jnp.concatenate([own[:, 0], left[:, :1], right[:, :1]], axis=1)
    up = lax.ppermute(last, "space", downward)
    down = lax.ppermute(start, "space", upward)
    sums = lax.all_to_all(jnp.broadcast_to(sums, (times, 1, 128)), "tm", 0, 0).reshape(times, 128)
    blank = jnp.zeros((count, 12, channels), BF16)
    edge = jnp.concatenate([left, right, up[:, :width], down[:, :width], up[:, width:], down[:, width:], blank], axis=1)
    past_edge = lax.ppermute(edge, "tm", later)

    taps = conv_filter.reshape(9, 3 * channels, channels)
    output = convolve(place, sums, own, past, edge, past_edge, norm_gain[None], norm_shift[None], taps,
                      conv_offset[None])
    return output[:, None]


def solution(mesh):
    placed = (P("tm", "space", None, None, None), P(), P(), P(), P())
    return jax.shard_map(
        local,
        mesh=mesh,
        in_specs=placed,
        out_specs=P("tm", "space", None, None, None),
        check_vma=False,
    )
```

```python
import functools

import jax
import jax.numpy as jnp
from jax import lax
from jax.experimental import pallas as pl
from jax.experimental.pallas import tpu as pltpu
from jax.sharding import PartitionSpec as P

GROUPS = 32
ACROSS = 4
F32, BF16 = jnp.float32, jnp.bfloat16
SMALL = pltpu.CompilerParams(vmem_limit_bytes=8 << 20)
LARGE = pltpu.CompilerParams(vmem_limit_bytes=60 << 20)
VMEM = pl.BlockSpec(memory_space=pltpu.VMEM)
SMEM = pl.BlockSpec(memory_space=pltpu.SMEM)
AWAY = pl.BlockSpec(memory_space=pltpu.HBM)


def in_hbm(array):
    return pltpu.with_memory_space_constraint(array, pltpu.HBM)


def cost(flops):
    return pl.CostEstimate(flops=flops, bytes_accessed=1 << 17, transcendentals=0)


def split(value):
    high = value.astype(BF16)
    rest = value - high.astype(F32)
    middle = rest.astype(BF16)
    low = (rest - middle.astype(F32)).astype(BF16)
    return high, middle, low


def exact_dot(value, table):
    return sum(jnp.dot(part, table, preferred_element_type=F32) for part in split(value))


def split_rows(row):
    high, middle, low = (part.astype(F32) for part in split(row))
    upper = jnp.concatenate([high, middle], axis=1)
    lower = jnp.concatenate([low, jnp.zeros_like(low)], axis=1)
    place = lax.broadcasted_iota(jnp.int32, (16, upper.shape[1]), 0)
    return jnp.where(place == 0, upper, jnp.where(place == 1, lower, 0.0))


def joined_row(block):
    upper, lower = block[0:1], block[1:2]
    return upper[:, :128] + upper[:, 128:] + lower[:, :128]


def sums_kernel(frames_hbm, gain_hbm, shift_hbm, offset_hbm, message_ref, columns_ref, gain_ref, shift_ref,
                offset_ref, arrived, *, frames):
    rows, width, channels = frames_hbm.shape
    height = rows // frames
    per_group = channels // GROUPS
    part = rows // 4
    fetches = []
    for at in range(4):
        span = pl.ds(at * part, part)
        fetches.append(pltpu.make_async_copy(frames_hbm.at[span], message_ref.at[span], arrived.at[at]))
        fetches[-1].start()
    small = ((gain_hbm, gain_ref), (shift_hbm, shift_ref), (offset_hbm, offset_ref))
    for at, (source, target) in enumerate(small):
        fetches.append(pltpu.make_async_copy(source, target, arrived.at[4 + at]))
        fetches[-1].start()
    message_ref[rows:] = jnp.zeros((message_ref.shape[0] - rows, width, channels), BF16)
    channel = lax.broadcasted_iota(jnp.int32, (channels, 128), 0)
    lane = lax.broadcasted_iota(jnp.int32, (channels, 128), 1)
    total = jnp.zeros((8, 128), F32)
    for frame in range(frames):
        plain = jnp.zeros((8, channels), F32)
        square = jnp.zeros((8, channels), F32)
        firsts, lasts = [], []
        for row in range(frame * height, (frame + 1) * height):
            if row % part == 0:
                fetches[row // part].wait()
            block = message_ref[row].astype(F32)
            firsts.append(block[0:1])
            lasts.append(block[width - 1 : width])
            block = block.reshape(width // 8, 8, channels)
            plain = plain + block.sum(0)
            square = square + (block * block).sum(0)
        for kind, value in enumerate((plain, square)):
            slot = (kind * frames + frame) * GROUPS
            table = jnp.where(lane == slot + channel // per_group, 1.0, 0.0).astype(BF16)
            total = total + exact_dot(value, table)
        columns_ref[frame * height : (frame + 1) * height] = jnp.concatenate(firsts, axis=0).astype(BF16)
        columns_ref[rows + frame * height : rows + (frame + 1) * height] = jnp.concatenate(lasts, axis=0).astype(BF16)
    columns_ref[2 * rows : 2 * rows + 16] = split_rows(total.sum(0, keepdims=True)).astype(BF16)
    for fetch in fetches[4:]:
        fetch.wait()


def group_sums(own, gain, shift, offset):
    count, height, width, channels = own.shape
    rows = count * height
    vector = jax.ShapeDtypeStruct(gain.shape, F32)
    return pl.pallas_call(
        functools.partial(sums_kernel, frames=count),
        out_shape=[
            jax.ShapeDtypeStruct((rows + 4 * count, width, channels), BF16),
            jax.ShapeDtypeStruct((2 * rows + 16, channels), BF16),
            vector,
            vector,
            vector,
        ],
        in_specs=[AWAY] * 4,
        out_specs=[VMEM] * 5,
        scratch_shapes=[pltpu.SemaphoreType.DMA((7,))],
        compiler_params=SMALL,
        cost_estimate=cost(1 << 20),
    )(in_hbm(own.reshape(rows, width, channels)), in_hbm(gain), in_hbm(shift), in_hbm(offset))


def beside(index, step, count):
    return jnp.clip(index + step, 0, count - 1)


def rows_kernel(place_ref, message_ref, sides_ref, out_ref, *, frames, height):
    width, channels = message_ref.shape[1:]
    members, receivers = sides_ref.shape[0], out_ref.shape[0]
    rows = frames * height
    row_of, col_of = place_ref[1] // ACROSS, place_ref[1] % ACROSS
    on_left, on_right = beside(col_of, -1, members), beside(col_of, 1, members)
    total = jnp.zeros((1, 128), F32)
    for member in range(members):
        total = total + joined_row(sides_ref[member, 2 * rows : 2 * rows + 16].astype(F32))
    upper = lower = split_rows(total)
    place = lax.broadcasted_iota(jnp.int32, (16, channels), 0)
    for frame in range(frames):
        left = sides_ref[on_left, rows + frame * height : rows + (frame + 1) * height].astype(F32)
        right = sides_ref[on_right, frame * height : (frame + 1) * height].astype(F32)
        for at, side in enumerate((left, right)):
            upper = jnp.where(place == 2 + 2 * frame + at, side[0:1], upper)
            lower = jnp.where(place == 2 + 2 * frame + at, side[height - 1 : height], lower)
    for receiver in range(receivers):
        is_above = receiver < row_of
        for frame in range(frames):
            row = frame * height + jnp.where(is_above, 0, height - 1)
            out_ref[receiver, frame * width : (frame + 1) * width] = message_ref[row]
        ends = jnp.where(is_above, upper, lower)
        out_ref[receiver, frames * width : frames * width + 16] = ends.astype(BF16)


def edge_rows(place, message, sides, frames, height, receivers):
    width, channels = message.shape[1:]
    return pl.pallas_call(
        functools.partial(rows_kernel, frames=frames, height=height),
        out_shape=jax.ShapeDtypeStruct((receivers, frames * width + 16, channels), BF16),
        in_specs=[SMEM, VMEM, VMEM],
        out_specs=VMEM,
        compiler_params=SMALL,
        cost_estimate=cost(1 << 20),
    )(place, message, sides)


def border_kernel(place_ref, message_ref, sides_ref, rows_ref, out_ref, sums_ref, *, frames, height):
    width, channels = message_ref.shape[1:]
    members, across = rows_ref.shape[0], sides_ref.shape[0]
    rows = frames * height
    row_of, col_of = place_ref[1] // ACROSS, place_ref[1] % ACROSS
    on_left, on_right = beside(col_of, -1, across), beside(col_of, 1, across)
    above, below = beside(row_of, -1, members), beside(row_of, 1, members)
    ends_at = frames * width
    total = jnp.zeros((1, 128), F32)
    for member in range(members):
        total = total + joined_row(rows_ref[member, ends_at : ends_at + 16].astype(F32))
    sums_ref[...] = jnp.broadcast_to(total[None], sums_ref.shape)
    upper = rows_ref[above, ends_at : ends_at + 16].astype(F32)
    lower = rows_ref[below, ends_at : ends_at + 16].astype(F32)
    place = lax.broadcasted_iota(jnp.int32, (16, channels), 0)
    for frame in range(frames):
        at = rows + 4 * frame
        out_ref[at, 0:height] = sides_ref[on_left, rows + frame * height : rows + (frame + 1) * height]
        out_ref[at, height : 2 * height] = sides_ref[on_right, frame * height : (frame + 1) * height]
        out_ref[at + 1] = rows_ref[above, frame * width : (frame + 1) * width]
        out_ref[at + 2] = rows_ref[below, frame * width : (frame + 1) * width]
        base = 2 + 2 * frame
        cells = (upper[base : base + 1], lower[base : base + 1], upper[base + 1 : base + 2], lower[base + 1 : base + 2])
        corners = jnp.zeros((16, channels), F32)
        for index, cell in enumerate(cells):
            corners = jnp.where(place == index, cell, corners)
        out_ref[at + 3, 0:16] = corners.astype(BF16)


def add_border(place, message, sides, rows, frames, height, receivers):
    return pl.pallas_call(
        functools.partial(border_kernel, frames=frames, height=height),
        out_shape=[
            jax.ShapeDtypeStruct(message.shape, BF16),
            jax.ShapeDtypeStruct((receivers, 1, 128), F32),
        ],
        in_specs=[SMEM, VMEM, VMEM, VMEM],
        out_specs=[VMEM, VMEM],
        input_output_aliases={1: 0},
        compiler_params=SMALL,
        cost_estimate=cost(1 << 20),
    )(place, message, sides, rows)


def norm_scales(sums, gain, time, cells):
    channels = gain.shape[1]
    per_group = channels // GROUPS
    index = lax.broadcasted_iota(jnp.int32, sums.shape, 0)
    lane = lax.broadcasted_iota(jnp.int32, (1, 128), 1)
    first = jnp.where((lane // GROUPS) % 2 == 0, 1.0, 0.0).astype(F32)
    before = jnp.where(index < time - 1, sums, 0.0).sum(0, keepdims=True)
    past = jnp.where(index == time - 1, sums, 0.0).sum(0, keepdims=True)
    own = jnp.where(index == time, sums, 0.0).sum(0, keepdims=True)
    running = jnp.concatenate(
        [before + past * first, before + past, before + past + own * first, before + past + own]
        + [jnp.zeros((4, 128), F32)],
        axis=0,
    )
    slot = lax.broadcasted_iota(jnp.int32, (128, channels), 0)
    channel = lax.broadcasted_iota(jnp.int32, (128, channels), 1)
    wide = []
    for kind in range(2):
        table = (slot // (2 * GROUPS) == kind) & (slot % GROUPS == channel // per_group)
        wide.append(exact_dot(running, jnp.where(table, 1.0, 0.0).astype(BF16)))
    frame_row = lax.broadcasted_iota(jnp.int32, (8, channels), 0)
    count = jnp.maximum((time * 2 - 1 + frame_row) * cells, 1).astype(F32)
    mean = wide[0] / count
    spread = wide[1] / count - mean * mean
    return mean, lax.rsqrt(spread + 1e-06) * gain


def conv_kernel(place_ref, sums_ref, past_ref, own_ref, gain_ref, shift_ref, offset_ref, filter_hbm, out_ref, shifted,
                taps_ref, arrived):
    fetch = pltpu.make_async_copy(filter_hbm, taps_ref, arrived)
    fetch.start()
    frames, height, width, channels = out_ref.shape
    rows = frames * height
    time, tile, tiles = place_ref[0], place_ref[1], place_ref[2]
    row_of, col_of = tile // ACROSS, tile % ACROSS
    down_max = tiles // ACROSS - 1
    mean, scale = norm_scales(sums_ref[...], gain_ref[...], time, height * width * tiles * (channels // GROUPS))
    shift = shift_ref[...]

    def activate(value, which):
        u = (value.astype(F32) - mean[which : which + 1]) * scale[which : which + 1] + shift
        return u / (1.0 + jnp.exp(-u))

    has_left = jnp.where(col_of > 0, 1.0, 0.0).astype(F32)
    has_right = jnp.where(col_of < ACROSS - 1, 1.0, 0.0).astype(F32)
    has_up = jnp.where(row_of > 0, 1.0, 0.0).astype(F32)
    has_down = jnp.where(row_of < down_max, 1.0, 0.0).astype(F32)
    has_past = jnp.where(time > 0, 1.0, 0.0).astype(F32)
    place = lax.broadcasted_iota(jnp.int32, (width, channels), 0)

    def put(which, row, center, left, right):
        at = pl.ds((which * (height + 2) + row) * width, width)
        toward = jnp.where(place == 0, left, pltpu.roll(center, 1, 0))
        away = jnp.where(place == width - 1, right, pltpu.roll(center, width - 1, 0))
        shifted[at, 0:channels] = toward.astype(BF16)
        shifted[at, channels : 2 * channels] = center.astype(BF16)
        shifted[at, 2 * channels : 3 * channels] = away.astype(BF16)

    def prepare(which):
        source = past_ref if which < 2 else own_ref
        here = has_past if which < 2 else jnp.ones((), F32)
        frame = which % 2
        at = rows + 4 * frame
        left = activate(source[at, 0:height], which) * (has_left * here)
        right = activate(source[at, height : 2 * height], which) * (has_right * here)
        up = activate(source[at + 1], which) * (has_up * here)
        down = activate(source[at + 2], which) * (has_down * here)
        corners = activate(source[at + 3, 0:16], which) * here
        put(which, 0, up, corners[0:1] * (has_up * has_left), corners[2:3] * (has_up * has_right))
        put(which, height + 1, down, corners[1:2] * (has_down * has_left), corners[3:4] * (has_down * has_right))
        for row in range(height):
            center = activate(source[frame * height + row], which)
            if which < 2:
                center = center * here
            put(which, row + 1, center, left[row : row + 1], right[row : row + 1])

    for which in range(4):
        prepare(which)
    fetch.wait()
    for frame in range(frames):
        total = jnp.zeros((height * width, channels), F32)
        for lagged in range(3):
            for vertical in range(3):
                at = ((frame + lagged) * (height + 2) + vertical) * width
                total = total + jnp.dot(
                    shifted[at : at + height * width, :],
                    taps_ref[lagged * 3 + vertical],
                    preferred_element_type=F32,
                )
        value = own_ref[frame * height : (frame + 1) * height].astype(F32).reshape(height * width, channels)
        value = value + (total + offset_ref[...])
        out_ref[frame] = value.astype(BF16).reshape(height, width, channels)


def convolve(place, sums, past, own, gain, shift, offset, taps, shape):
    frames, height, width, channels = shape
    return pl.pallas_call(
        conv_kernel,
        out_shape=jax.ShapeDtypeStruct(shape, BF16),
        in_specs=[SMEM, VMEM, VMEM, VMEM, VMEM, VMEM, VMEM, AWAY],
        out_specs=VMEM,
        scratch_shapes=[
            pltpu.VMEM((4 * (height + 2) * width, 3 * channels), BF16),
            pltpu.VMEM(taps.shape, BF16),
            pltpu.SemaphoreType.DMA(()),
        ],
        compiler_params=pltpu.CompilerParams(vmem_limit_bytes=32 << 20),
        cost_estimate=pl.CostEstimate(flops=4 << 30, bytes_accessed=6 << 20, transcendentals=1 << 20),
    )(place, sums, past, own, gain, shift, offset, in_hbm(taps))


def local(frames, norm_gain, norm_shift, conv_filter, conv_offset):
    own = frames[:, 0]
    count, height, width, channels = own.shape
    times, tiles = lax.axis_size("tm"), lax.axis_size("space")
    place = jnp.stack([lax.axis_index("tm"), lax.axis_index("space"), jnp.int32(tiles)]).astype(jnp.int32)

    later = [(t, t + 1) for t in range(times - 1)]
    across = [[row + col for col in range(ACROSS)] for row in range(0, tiles, ACROSS)]
    along = [[row + col for row in range(0, tiles, ACROSS)] for col in range(ACROSS)]

    message, columns, gain, shift, offset = group_sums(own, norm_gain[None], norm_shift[None], conv_offset[None])
    sides = lax.all_gather(columns, "space", axis_index_groups=across)
    rows = edge_rows(place, message, sides, count, height, tiles // ACROSS)
    rows = lax.all_to_all(rows, "space", 0, 0, axis_index_groups=along)
    message, sums = add_border(place, message, sides, rows, count, height, times)
    past = lax.ppermute(message, "tm", later)
    sums = lax.all_to_all(sums, "tm", 0, 0).reshape(times, 128)

    taps = conv_filter.reshape(9, 3 * channels, channels)
    output = convolve(place, sums, past, message, gain, shift, offset, taps, own.shape)
    return output[:, None]


def solution(mesh):
    placed = (P("tm", "space", None, None, None), P(), P(), P(), P())
    return jax.shard_map(
        local,
        mesh=mesh,
        in_specs=placed,
        out_specs=P("tm", "space", None, None, None),
        check_vma=False,
    )
```

```python
import functools

import jax
import jax.numpy as jnp
from jax import lax
from jax.experimental import pallas as pl
from jax.experimental.pallas import tpu as pltpu
from jax.sharding import PartitionSpec as P

GROUPS = 32
ACROSS = 4
F32, BF16 = jnp.float32, jnp.bfloat16
SMALL = pltpu.CompilerParams(vmem_limit_bytes=8 << 20)
VMEM = pl.BlockSpec(memory_space=pltpu.VMEM)
AWAY = pl.BlockSpec(memory_space=pltpu.HBM)


def in_vmem(array):
    return pltpu.with_memory_space_constraint(array, pltpu.VMEM)


def in_hbm(array):
    return pltpu.with_memory_space_constraint(array, pltpu.HBM)


def cost(flops):
    return pl.CostEstimate(flops=flops, bytes_accessed=1 << 17, transcendentals=0)


def split(value):
    high = value.astype(BF16)
    rest = value - high.astype(F32)
    middle = rest.astype(BF16)
    low = (rest - middle.astype(F32)).astype(BF16)
    return high, middle, low


def exact_dot(value, table):
    return sum(jnp.dot(part, table, preferred_element_type=F32) for part in split(value))


def split_rows(row):
    high, middle, low = (part.astype(F32) for part in split(row))
    upper = jnp.concatenate([high, middle], axis=1)
    lower = jnp.concatenate([low, jnp.zeros_like(low)], axis=1)
    place = lax.broadcasted_iota(jnp.int32, (16, upper.shape[1]), 0)
    return jnp.where(place == 0, upper, jnp.where(place == 1, lower, 0.0))


def joined_row(block):
    upper, lower = block[0:1], block[1:2]
    return upper[:, :128] + upper[:, 128:] + lower[:, :128]


def sums_kernel(frames_hbm, gain_hbm, shift_hbm, offset_hbm, message_ref, columns_ref, gain_ref, shift_ref,
                offset_ref, arrived, *, frames):
    rows, width, channels = frames_hbm.shape
    height = rows // frames
    per_group = channels // GROUPS
    part = rows // 4
    fetches = []
    for at in range(4):
        span = pl.ds(at * part, part)
        fetches.append(pltpu.make_async_copy(frames_hbm.at[span], message_ref.at[span], arrived.at[at]))
        fetches[-1].start()
    small = ((gain_hbm, gain_ref), (shift_hbm, shift_ref), (offset_hbm, offset_ref))
    for at, (source, target) in enumerate(small):
        fetches.append(pltpu.make_async_copy(source, target, arrived.at[4 + at]))
        fetches[-1].start()
    message_ref[rows:] = jnp.zeros((message_ref.shape[0] - rows, width, channels), BF16)
    channel = lax.broadcasted_iota(jnp.int32, (channels, 128), 0)
    lane = lax.broadcasted_iota(jnp.int32, (channels, 128), 1)
    total = jnp.zeros((8, 128), F32)
    for frame in range(frames):
        plain = jnp.zeros((8, channels), F32)
        square = jnp.zeros((8, channels), F32)
        firsts, lasts = [], []
        for row in range(frame * height, (frame + 1) * height):
            if row % part == 0:
                fetches[row // part].wait()
            block = message_ref[row].astype(F32)
            firsts.append(block[0:1])
            lasts.append(block[width - 1 : width])
            block = block.reshape(width // 8, 8, channels)
            plain = plain + block.sum(0)
            square = square + (block * block).sum(0)
        for kind, value in enumerate((plain, square)):
            slot = (kind * frames + frame) * GROUPS
            table = jnp.where(lane == slot + channel // per_group, 1.0, 0.0).astype(BF16)
            total = total + exact_dot(value, table)
        columns_ref[frame * height : (frame + 1) * height] = jnp.concatenate(firsts, axis=0).astype(BF16)
        columns_ref[rows + frame * height : rows + (frame + 1) * height] = jnp.concatenate(lasts, axis=0).astype(BF16)
    columns_ref[2 * rows : 2 * rows + 16] = split_rows(total.sum(0, keepdims=True)).astype(BF16)
    for fetch in fetches[4:]:
        fetch.wait()


def group_sums(own, gain, shift, offset):
    count, height, width, channels = own.shape
    rows = count * height
    vector = jax.ShapeDtypeStruct(gain.shape, F32)
    return pl.pallas_call(
        functools.partial(sums_kernel, frames=count),
        out_shape=[
            jax.ShapeDtypeStruct((rows + 4 * count, width, channels), BF16),
            jax.ShapeDtypeStruct((2 * rows + 16, channels), BF16),
            vector,
            vector,
            vector,
        ],
        in_specs=[AWAY] * 4,
        out_specs=[VMEM] * 5,
        scratch_shapes=[pltpu.SemaphoreType.DMA((7,))],
        compiler_params=SMALL,
        cost_estimate=cost(1 << 20),
    )(in_hbm(own.reshape(rows, width, channels)), in_hbm(gain), in_hbm(shift), in_hbm(offset))


def beside(index, step, count):
    return jnp.clip(index + step, 0, count - 1)


def rows_kernel(message_ref, sides_ref, taps_hbm, out_ref, *, frames, height):
    width, channels = message_ref.shape[1:]
    members, receivers = sides_ref.shape[0], out_ref.shape[0]
    rows = frames * height
    tile = lax.axis_index("space")
    row_of, col_of = tile // ACROSS, tile % ACROSS
    on_left, on_right = beside(col_of, -1, members), beside(col_of, 1, members)
    total = jnp.zeros((1, 128), F32)
    for member in range(members):
        total = total + joined_row(sides_ref[member, 2 * rows : 2 * rows + 16].astype(F32))
    upper = lower = split_rows(total)
    place = lax.broadcasted_iota(jnp.int32, (16, channels), 0)
    for frame in range(frames):
        left = sides_ref[on_left, rows + frame * height : rows + (frame + 1) * height].astype(F32)
        right = sides_ref[on_right, frame * height : (frame + 1) * height].astype(F32)
        for at, side in enumerate((left, right)):
            upper = jnp.where(place == 2 + 2 * frame + at, side[0:1], upper)
            lower = jnp.where(place == 2 + 2 * frame + at, side[height - 1 : height], lower)
    for receiver in range(receivers):
        is_above = receiver < row_of
        for frame in range(frames):
            row = frame * height + jnp.where(is_above, 0, height - 1)
            out_ref[receiver, frame * width : (frame + 1) * width] = message_ref[row]
        ends = jnp.where(is_above, upper, lower)
        out_ref[receiver, frames * width : frames * width + 16] = ends.astype(BF16)


def edge_rows(message, sides, taps, frames, height, receivers):
    width, channels = message.shape[1:]
    return pl.pallas_call(
        functools.partial(rows_kernel, frames=frames, height=height),
        out_shape=jax.ShapeDtypeStruct((receivers, frames * width + 16, channels), BF16),
        in_specs=[VMEM, VMEM, AWAY],
        out_specs=VMEM,
        compiler_params=SMALL,
        cost_estimate=cost(1 << 20),
    )(message, sides, in_hbm(taps))


def border_kernel(message_ref, sides_ref, rows_ref, out_ref, sums_ref, *, frames, height):
    width, channels = message_ref.shape[1:]
    members, across = rows_ref.shape[0], sides_ref.shape[0]
    rows = frames * height
    tile = lax.axis_index("space")
    row_of, col_of = tile // ACROSS, tile % ACROSS
    on_left, on_right = beside(col_of, -1, across), beside(col_of, 1, across)
    above, below = beside(row_of, -1, members), beside(row_of, 1, members)
    ends_at = frames * width
    total = jnp.zeros((1, 128), F32)
    for member in range(members):
        total = total + joined_row(rows_ref[member, ends_at : ends_at + 16].astype(F32))
    sums_ref[...] = jnp.broadcast_to(total[None], sums_ref.shape)
    upper = rows_ref[above, ends_at : ends_at + 16].astype(F32)
    lower = rows_ref[below, ends_at : ends_at + 16].astype(F32)
    place = lax.broadcasted_iota(jnp.int32, (16, channels), 0)
    for frame in range(frames):
        at = rows + 4 * frame
        out_ref[at, 0:height] = sides_ref[on_left, rows + frame * height : rows + (frame + 1) * height]
        out_ref[at, height : 2 * height] = sides_ref[on_right, frame * height : (frame + 1) * height]
        out_ref[at + 1] = rows_ref[above, frame * width : (frame + 1) * width]
        out_ref[at + 2] = rows_ref[below, frame * width : (frame + 1) * width]
        base = 2 + 2 * frame
        cells = (upper[base : base + 1], lower[base : base + 1], upper[base + 1 : base + 2], lower[base + 1 : base + 2])
        corners = jnp.zeros((16, channels), F32)
        for index, cell in enumerate(cells):
            corners = jnp.where(place == index, cell, corners)
        out_ref[at + 3, 0:16] = corners.astype(BF16)


def add_border(message, sides, rows, frames, height, receivers):
    return pl.pallas_call(
        functools.partial(border_kernel, frames=frames, height=height),
        out_shape=[
            jax.ShapeDtypeStruct(message.shape, BF16),
            jax.ShapeDtypeStruct((receivers, 1, 128), F32),
        ],
        in_specs=[VMEM, VMEM, VMEM],
        out_specs=[VMEM, VMEM],
        input_output_aliases={0: 0},
        compiler_params=SMALL,
        cost_estimate=cost(1 << 20),
    )(message, sides, rows)


def norm_scales(sums, gain, time, cells):
    channels = gain.shape[1]
    per_group = channels // GROUPS
    index = lax.broadcasted_iota(jnp.int32, sums.shape, 0)
    lane = lax.broadcasted_iota(jnp.int32, (1, 128), 1)
    first = jnp.where((lane // GROUPS) % 2 == 0, 1.0, 0.0).astype(F32)
    before = jnp.where(index < time - 1, sums, 0.0).sum(0, keepdims=True)
    past = jnp.where(index == time - 1, sums, 0.0).sum(0, keepdims=True)
    own = jnp.where(index == time, sums, 0.0).sum(0, keepdims=True)
    running = jnp.concatenate(
        [before + past * first, before + past, before + past + own * first, before + past + own]
        + [jnp.zeros((4, 128), F32)],
        axis=0,
    )
    slot = lax.broadcasted_iota(jnp.int32, (128, channels), 0)
    channel = lax.broadcasted_iota(jnp.int32, (128, channels), 1)
    wide = []
    for kind in range(2):
        table = (slot // (2 * GROUPS) == kind) & (slot % GROUPS == channel // per_group)
        wide.append(exact_dot(running, jnp.where(table, 1.0, 0.0).astype(BF16)))
    frame_row = lax.broadcasted_iota(jnp.int32, (8, channels), 0)
    count = jnp.maximum((time * 2 - 1 + frame_row) * cells, 1).astype(F32)
    mean = wide[0] / count
    spread = wide[1] / count - mean * mean
    return mean, lax.rsqrt(spread + 1e-06) * gain


def conv_kernel(sums_ref, past_ref, own_ref, gain_ref, shift_ref, offset_ref, taps_ref, out_ref, shifted):
    frames, height, width, channels = out_ref.shape
    rows = frames * height
    time, tile, tiles = lax.axis_index("tm"), lax.axis_index("space"), lax.axis_size("space")
    row_of, col_of = tile // ACROSS, tile % ACROSS
    down_max = tiles // ACROSS - 1
    mean, scale = norm_scales(sums_ref[...], gain_ref[...], time, height * width * tiles * (channels // GROUPS))
    shift = shift_ref[...]

    def activate(value, which):
        u = (value.astype(F32) - mean[which : which + 1]) * scale[which : which + 1] + shift
        return u / (1.0 + jnp.exp(-u))

    has_left = jnp.where(col_of > 0, 1.0, 0.0).astype(F32)
    has_right = jnp.where(col_of < ACROSS - 1, 1.0, 0.0).astype(F32)
    has_up = jnp.where(row_of > 0, 1.0, 0.0).astype(F32)
    has_down = jnp.where(row_of < down_max, 1.0, 0.0).astype(F32)
    has_past = jnp.where(time > 0, 1.0, 0.0).astype(F32)
    place = lax.broadcasted_iota(jnp.int32, (width, channels), 0)

    def put(which, row, center, left, right):
        at = pl.ds((which * (height + 2) + row) * width, width)
        toward = jnp.where(place == 0, left, pltpu.roll(center, 1, 0))
        away = jnp.where(place == width - 1, right, pltpu.roll(center, width - 1, 0))
        shifted[at, 0:channels] = toward.astype(BF16)
        shifted[at, channels : 2 * channels] = center.astype(BF16)
        shifted[at, 2 * channels : 3 * channels] = away.astype(BF16)

    def prepare(which):
        source = past_ref if which < 2 else own_ref
        here = has_past if which < 2 else jnp.ones((), F32)
        frame = which % 2
        at = rows + 4 * frame
        left = activate(source[at, 0:height], which) * (has_left * here)
        right = activate(source[at, height : 2 * height], which) * (has_right * here)
        up = activate(source[at + 1], which) * (has_up * here)
        down = activate(source[at + 2], which) * (has_down * here)
        corners = activate(source[at + 3, 0:16], which) * here
        put(which, 0, up, corners[0:1] * (has_up * has_left), corners[2:3] * (has_up * has_right))
        put(which, height + 1, down, corners[1:2] * (has_down * has_left), corners[3:4] * (has_down * has_right))
        for row in range(height):
            center = activate(source[frame * height + row], which)
            if which < 2:
                center = center * here
            put(which, row + 1, center, left[row : row + 1], right[row : row + 1])

    for which in range(4):
        prepare(which)
    for frame in range(frames):
        total = jnp.zeros((height * width, channels), F32)
        for lagged in range(3):
            for vertical in range(3):
                at = ((frame + lagged) * (height + 2) + vertical) * width
                total = total + jnp.dot(
                    shifted[at : at + height * width, :],
                    taps_ref[lagged * 3 + vertical],
                    preferred_element_type=F32,
                )
        value = own_ref[frame * height : (frame + 1) * height].astype(F32).reshape(height * width, channels)
        value = value + (total + offset_ref[...])
        out_ref[frame] = value.astype(BF16).reshape(height, width, channels)


def convolve(sums, past, own, gain, shift, offset, taps, shape):
    frames, height, width, channels = shape
    return pl.pallas_call(
        conv_kernel,
        out_shape=jax.ShapeDtypeStruct(shape, BF16),
        in_specs=[VMEM] * 7,
        out_specs=VMEM,
        scratch_shapes=[
            pltpu.VMEM((4 * (height + 2) * width, 3 * channels), BF16),
        ],
        compiler_params=pltpu.CompilerParams(vmem_limit_bytes=32 << 20),
        cost_estimate=pl.CostEstimate(flops=4 << 30, bytes_accessed=6 << 20, transcendentals=1 << 20),
    )(sums, past, own, gain, shift, offset, in_vmem(taps))


def local(frames, norm_gain, norm_shift, conv_filter, conv_offset):
    own = frames[:, 0]
    count, height, width, channels = own.shape
    times, tiles = lax.axis_size("tm"), lax.axis_size("space")

    later = [(t, t + 1) for t in range(times - 1)]
    across = [[row + col for col in range(ACROSS)] for row in range(0, tiles, ACROSS)]
    along = [[row + col for row in range(0, tiles, ACROSS)] for col in range(ACROSS)]

    message, columns, gain, shift, offset = group_sums(own, norm_gain[None], norm_shift[None], conv_offset[None])
    sides = lax.all_gather(columns, "space", axis_index_groups=across)
    taps = conv_filter.reshape(9, 3 * channels, channels)
    rows = edge_rows(message, sides, taps, count, height, tiles // ACROSS)
    rows = lax.all_to_all(rows, "space", 0, 0, axis_index_groups=along)
    message, sums = add_border(message, sides, rows, count, height, times)
    past = lax.ppermute(message, "tm", later)
    sums = lax.all_to_all(sums, "tm", 0, 0).reshape(times, 128)

    taps = conv_filter.reshape(9, 3 * channels, channels)
    output = convolve(sums, past, message, gain, shift, offset, taps, own.shape)
    return output[:, None]


def solution(mesh):
    placed = (P("tm", "space", None, None, None), P(), P(), P(), P())
    return jax.shard_map(
        local,
        mesh=mesh,
        in_specs=placed,
        out_specs=P("tm", "space", None, None, None),
        check_vma=False,
    )
```

```python
import functools

import jax
import jax.numpy as jnp
from jax import lax
from jax.experimental import pallas as pl
from jax.experimental.pallas import tpu as pltpu
from jax.sharding import PartitionSpec as P

GROUPS = 32
ACROSS = 4
F32, BF16 = jnp.float32, jnp.bfloat16
SMALL = pltpu.CompilerParams(vmem_limit_bytes=8 << 20)
VMEM = pl.BlockSpec(memory_space=pltpu.VMEM)
AWAY = pl.BlockSpec(memory_space=pltpu.HBM)


def in_vmem(array):
    return pltpu.with_memory_space_constraint(array, pltpu.VMEM)


def in_hbm(array):
    return pltpu.with_memory_space_constraint(array, pltpu.HBM)


def cost(flops):
    return pl.CostEstimate(flops=flops, bytes_accessed=1 << 17, transcendentals=0)


def split(value):
    high = value.astype(BF16)
    rest = value - high.astype(F32)
    middle = rest.astype(BF16)
    low = (rest - middle.astype(F32)).astype(BF16)
    return high, middle, low


def exact_dot(value, table):
    parts = jnp.concatenate([part.astype(F32) for part in split(value)] + [jnp.zeros_like(value)], axis=0)
    product = jnp.dot(parts.astype(BF16), table.astype(BF16), preferred_element_type=F32)
    return product[0:8] + (product[8:16] + product[16:24])


def split_rows(row):
    high, middle, low = (part.astype(F32) for part in split(row))
    upper = jnp.concatenate([high, middle], axis=1)
    lower = jnp.concatenate([low, jnp.zeros_like(low)], axis=1)
    place = lax.broadcasted_iota(jnp.int32, (16, upper.shape[1]), 0)
    return jnp.where(place == 0, upper, jnp.where(place == 1, lower, 0.0))


def joined_row(block):
    upper, lower = block[0:1], block[1:2]
    return upper[:, :128] + upper[:, 128:] + lower[:, :128]


def sums_kernel(frames_hbm, gain_hbm, shift_hbm, offset_hbm, message_ref, columns_ref, gain_ref, shift_ref,
                offset_ref, arrived, *, frames):
    rows, width, channels = frames_hbm.shape
    height = rows // frames
    per_group = channels // GROUPS
    part = rows // 4
    fetches = []
    for at in range(4):
        span = pl.ds(at * part, part)
        fetches.append(pltpu.make_async_copy(frames_hbm.at[span], message_ref.at[span], arrived.at[at]))
        fetches[-1].start()
    small = ((gain_hbm, gain_ref), (shift_hbm, shift_ref), (offset_hbm, offset_ref))
    for at, (source, target) in enumerate(small):
        fetches.append(pltpu.make_async_copy(source, target, arrived.at[4 + at]))
        fetches[-1].start()
    message_ref[rows:] = jnp.zeros((message_ref.shape[0] - rows, width, channels), BF16)
    kinds = 2 * frames
    source = lax.broadcasted_iota(jnp.int32, (kinds * channels, 128), 0)
    lane = lax.broadcasted_iota(jnp.int32, (kinds * channels, 128), 1)
    table = jnp.where(lane == source // per_group, 1.0, 0.0)
    plains, squares = [], []
    for frame in range(frames):
        plain = jnp.zeros((8, channels), F32)
        square = jnp.zeros((8, channels), F32)
        firsts, lasts = [], []
        for row in range(frame * height, (frame + 1) * height):
            if row % part == 0:
                fetches[row // part].wait()
            block = message_ref[row].astype(F32)
            firsts.append(block[0:1])
            lasts.append(block[width - 1 : width])
            block = block.reshape(width // 8, 8, channels)
            plain = plain + block.sum(0)
            square = square + (block * block).sum(0)
        plains.append(plain)
        squares.append(square)
        columns_ref[frame * height : (frame + 1) * height] = jnp.concatenate(firsts, axis=0).astype(BF16)
        columns_ref[rows + frame * height : rows + (frame + 1) * height] = jnp.concatenate(lasts, axis=0).astype(BF16)
    total = exact_dot(jnp.concatenate(plains + squares, axis=1), table)
    columns_ref[2 * rows : 2 * rows + 16] = split_rows(total.sum(0, keepdims=True)).astype(BF16)
    for fetch in fetches[4:]:
        fetch.wait()


def group_sums(own, gain, shift, offset):
    count, height, width, channels = own.shape
    rows = count * height
    vector = jax.ShapeDtypeStruct(gain.shape, F32)
    return pl.pallas_call(
        functools.partial(sums_kernel, frames=count),
        out_shape=[
            jax.ShapeDtypeStruct((rows + 3 * count + 1, width, channels), BF16),
            jax.ShapeDtypeStruct((2 * rows + 16, channels), BF16),
            vector,
            vector,
            vector,
        ],
        in_specs=[AWAY] * 4,
        out_specs=[VMEM] * 5,
        scratch_shapes=[pltpu.SemaphoreType.DMA((7,))],
        compiler_params=SMALL,
        cost_estimate=cost(1 << 20),
    )(in_hbm(own.reshape(rows, width, channels)), in_hbm(gain), in_hbm(shift), in_hbm(offset))


def beside(index, step, count):
    return jnp.clip(index + step, 0, count - 1)


def rows_kernel(message_ref, sides_ref, taps_hbm, out_ref, *, frames, height):
    width, channels = message_ref.shape[1:]
    members, receivers = sides_ref.shape[0], out_ref.shape[0]
    rows = frames * height
    tile = lax.axis_index("space")
    row_of, col_of = tile // ACROSS, tile % ACROSS
    on_left, on_right = beside(col_of, -1, members), beside(col_of, 1, members)
    total = jnp.zeros((1, 128), F32)
    for member in range(members):
        total = total + joined_row(sides_ref[member, 2 * rows : 2 * rows + 16].astype(F32))
    upper = lower = split_rows(total)
    place = lax.broadcasted_iota(jnp.int32, (16, channels), 0)
    for frame in range(frames):
        left = sides_ref[on_left, rows + frame * height : rows + (frame + 1) * height].astype(F32)
        right = sides_ref[on_right, frame * height : (frame + 1) * height].astype(F32)
        for at, side in enumerate((left, right)):
            upper = jnp.where(place == 2 + 2 * frame + at, side[0:1], upper)
            lower = jnp.where(place == 2 + 2 * frame + at, side[height - 1 : height], lower)
    for receiver in range(receivers):
        is_above = receiver < row_of
        for frame in range(frames):
            row = frame * height + jnp.where(is_above, 0, height - 1)
            out_ref[receiver, frame * width : (frame + 1) * width] = message_ref[row]
        ends = jnp.where(is_above, upper, lower)
        out_ref[receiver, frames * width : frames * width + 16] = ends.astype(BF16)


def edge_rows(message, sides, taps, frames, height, receivers):
    width, channels = message.shape[1:]
    return pl.pallas_call(
        functools.partial(rows_kernel, frames=frames, height=height),
        out_shape=jax.ShapeDtypeStruct((receivers, frames * width + 16, channels), BF16),
        in_specs=[VMEM, VMEM, AWAY],
        out_specs=VMEM,
        compiler_params=SMALL,
        cost_estimate=cost(1 << 20),
    )(message, sides, in_hbm(taps))


def border_kernel(message_ref, sides_ref, rows_ref, out_ref, sums_ref, *, frames, height):
    width, channels = message_ref.shape[1:]
    members, across = rows_ref.shape[0], sides_ref.shape[0]
    rows = frames * height
    tile = lax.axis_index("space")
    row_of, col_of = tile // ACROSS, tile % ACROSS
    on_left, on_right = beside(col_of, -1, across), beside(col_of, 1, across)
    above, below = beside(row_of, -1, members), beside(row_of, 1, members)
    ends_at = frames * width
    total = jnp.zeros((1, 128), F32)
    for member in range(members):
        total = total + joined_row(rows_ref[member, ends_at : ends_at + 16].astype(F32))
    sums_ref[...] = jnp.broadcast_to(total[None], sums_ref.shape)
    upper = rows_ref[above, ends_at : ends_at + 16].astype(F32)
    lower = rows_ref[below, ends_at : ends_at + 16].astype(F32)
    place = lax.broadcasted_iota(jnp.int32, (16, channels), 0)
    corners = jnp.zeros((16, channels), F32)
    for frame in range(frames):
        at = rows + 3 * frame
        out_ref[at, 0:height] = sides_ref[on_left, rows + frame * height : rows + (frame + 1) * height]
        out_ref[at, height : 2 * height] = sides_ref[on_right, frame * height : (frame + 1) * height]
        out_ref[at + 1] = rows_ref[above, frame * width : (frame + 1) * width]
        out_ref[at + 2] = rows_ref[below, frame * width : (frame + 1) * width]
        base = 2 + 2 * frame
        cells = (upper[base : base + 1], lower[base : base + 1], upper[base + 1 : base + 2], lower[base + 1 : base + 2])
        for index, cell in enumerate(cells):
            corners = jnp.where(place == 4 * frame + index, cell, corners)
    out_ref[rows + 3 * frames, 0:16] = corners.astype(BF16)


def add_border(message, sides, rows, frames, height, receivers):
    return pl.pallas_call(
        functools.partial(border_kernel, frames=frames, height=height),
        out_shape=[
            jax.ShapeDtypeStruct(message.shape, BF16),
            jax.ShapeDtypeStruct((receivers, 1, 128), F32),
        ],
        in_specs=[VMEM, VMEM, VMEM],
        out_specs=[VMEM, VMEM],
        input_output_aliases={0: 0},
        compiler_params=SMALL,
        cost_estimate=cost(1 << 20),
    )(message, sides, rows)


def norm_scales(sums, gain, time, cells):
    channels = gain.shape[1]
    per_group = channels // GROUPS
    index = lax.broadcasted_iota(jnp.int32, sums.shape, 0)
    lane = lax.broadcasted_iota(jnp.int32, (1, 128), 1)
    first = jnp.where((lane // GROUPS) % 2 == 0, 1.0, 0.0).astype(F32)
    before = jnp.where(index < time - 1, sums, 0.0).sum(0, keepdims=True)
    past = jnp.where(index == time - 1, sums, 0.0).sum(0, keepdims=True)
    own = jnp.where(index == time, sums, 0.0).sum(0, keepdims=True)
    running = jnp.concatenate(
        [before + past * first, before + past, before + past + own * first, before + past + own]
        + [jnp.zeros((4, 128), F32)],
        axis=0,
    )
    slot = lax.broadcasted_iota(jnp.int32, (128, 2 * channels), 0)
    target = lax.broadcasted_iota(jnp.int32, (128, 2 * channels), 1)
    table = (slot // (2 * GROUPS) == target // channels) & (slot % GROUPS == target % channels // per_group)
    wide = exact_dot(running, jnp.where(table, 1.0, 0.0))
    frame_row = lax.broadcasted_iota(jnp.int32, (8, channels), 0)
    count = jnp.maximum((time * 2 - 1 + frame_row) * cells, 1).astype(F32)
    mean = wide[:, :channels] / count
    spread = wide[:, channels:] / count - mean * mean
    return mean, lax.rsqrt(spread + 1e-06) * gain


def conv_kernel(sums_ref, past_ref, own_ref, gain_ref, shift_ref, offset_ref, taps_ref, out_hbm, shifted,
                out_ref, sent):
    frames, height, width, channels = out_ref.shape
    rows = frames * height
    time, tile, tiles = lax.axis_index("tm"), lax.axis_index("space"), lax.axis_size("space")
    row_of, col_of = tile // ACROSS, tile % ACROSS
    down_max = tiles // ACROSS - 1
    mean, scale = norm_scales(sums_ref[...], gain_ref[...], time, height * width * tiles * (channels // GROUPS))
    shift = shift_ref[...]

    def activate(value, which):
        u = (value.astype(F32) - mean[which : which + 1]) * scale[which : which + 1] + shift
        return u / (1.0 + jnp.exp(-u))

    has_left = jnp.where(col_of > 0, 1.0, 0.0).astype(F32)
    has_right = jnp.where(col_of < ACROSS - 1, 1.0, 0.0).astype(F32)
    has_up = jnp.where(row_of > 0, 1.0, 0.0).astype(F32)
    has_down = jnp.where(row_of < down_max, 1.0, 0.0).astype(F32)
    has_past = jnp.where(time > 0, 1.0, 0.0).astype(F32)
    place = lax.broadcasted_iota(jnp.int32, (width, channels), 0)

    def put(which, row, center, left, right):
        at = pl.ds((which * (height + 2) + row) * width, width)
        toward = jnp.where(place == 0, left, pltpu.roll(center, 1, 0))
        away = jnp.where(place == width - 1, right, pltpu.roll(center, width - 1, 0))
        shifted[at, 0:channels] = toward.astype(BF16)
        shifted[at, channels : 2 * channels] = center.astype(BF16)
        shifted[at, 2 * channels : 3 * channels] = away.astype(BF16)

    def prepare(which):
        source = past_ref if which < 2 else own_ref
        here = has_past if which < 2 else jnp.ones((), F32)
        frame = which % 2
        at = rows + 3 * frame
        left = activate(source[at, 0:height], which) * (has_left * here)
        right = activate(source[at, height : 2 * height], which) * (has_right * here)
        up = activate(source[at + 1], which) * (has_up * here)
        down = activate(source[at + 2], which) * (has_down * here)
        corners = activate(source[rows + 3 * frames, 0:16], which) * here
        corners = corners[4 * frame : 4 * frame + 4]
        put(which, 0, up, corners[0:1] * (has_up * has_left), corners[2:3] * (has_up * has_right))
        put(which, height + 1, down, corners[1:2] * (has_down * has_left), corners[3:4] * (has_down * has_right))
        for row in range(height):
            center = activate(source[frame * height + row], which)
            if which < 2:
                center = center * here
            put(which, row + 1, center, left[row : row + 1], right[row : row + 1])

    pieces = 4
    size = height * width // pieces
    totals = {}
    sends = []

    def gather(which):
        for frame in range(frames):
            lagged = which - frame
            if not 0 <= lagged < 3:
                continue
            for piece in range(pieces):
                for vertical in range(3):
                    at = (which * (height + 2) + vertical) * width + piece * size
                    part = jnp.dot(
                        shifted[at : at + size, :], taps_ref[lagged * 3 + vertical], preferred_element_type=F32
                    )
                    totals[frame, piece] = totals[frame, piece] + part if (frame, piece) in totals else part
                if lagged == 2:
                    finish(frame, piece)

    def finish(frame, piece):
        span = height // pieces
        value = own_ref[frame * height + piece * span : frame * height + (piece + 1) * span]
        value = value.astype(F32).reshape(size, channels) + (totals[frame, piece] + offset_ref[...])
        rows = pl.ds(piece * span, span)
        out_ref[frame, rows] = value.astype(BF16).reshape(span, width, channels)
        sends.append(pltpu.make_async_copy(
            out_ref.at[frame, rows], out_hbm.at[frame, rows], sent.at[frame * pieces + piece]))
        sends[-1].start()

    for which in range(4):
        prepare(which)
        gather(which)
    for send in sends:
        send.wait()


def convolve(sums, past, own, gain, shift, offset, taps, shape):
    frames, height, width, channels = shape
    return pl.pallas_call(
        conv_kernel,
        out_shape=pltpu.HBM(shape, BF16),
        in_specs=[VMEM] * 7,
        out_specs=AWAY,
        scratch_shapes=[
            pltpu.VMEM((4 * (height + 2) * width, 3 * channels), BF16),
            pltpu.VMEM(shape, BF16),
            pltpu.SemaphoreType.DMA((4 * frames,)),
        ],
        compiler_params=pltpu.CompilerParams(vmem_limit_bytes=32 << 20),
        cost_estimate=pl.CostEstimate(flops=4 << 30, bytes_accessed=6 << 20, transcendentals=1 << 20),
    )(sums, past, own, gain, shift, offset, in_vmem(taps))


def local(frames, norm_gain, norm_shift, conv_filter, conv_offset):
    own = frames[:, 0]
    count, height, width, channels = own.shape
    times, tiles = lax.axis_size("tm"), lax.axis_size("space")

    later = [(t, t + 1) for t in range(times - 1)]
    across = [[row + col for col in range(ACROSS)] for row in range(0, tiles, ACROSS)]
    along = [[row + col for row in range(0, tiles, ACROSS)] for col in range(ACROSS)]

    message, columns, gain, shift, offset = group_sums(own, norm_gain[None], norm_shift[None], conv_offset[None])
    sides = lax.all_gather(columns, "space", axis_index_groups=across)
    taps = conv_filter.reshape(9, 3 * channels, channels)
    rows = edge_rows(message, sides, taps, count, height, tiles // ACROSS)
    rows = lax.all_to_all(rows, "space", 0, 0, axis_index_groups=along)
    message, sums = add_border(message, sides, rows, count, height, times)
    past = lax.ppermute(message, "tm", later)
    sums = lax.all_to_all(sums, "tm", 0, 0).reshape(times, 128)

    taps = conv_filter.reshape(9, 3 * channels, channels)
    output = convolve(sums, past, message, gain, shift, offset, taps, own.shape)
    return output[:, None]


def solution(mesh):
    placed = (P("tm", "space", None, None, None), P(), P(), P(), P())
    return jax.shard_map(
        local,
        mesh=mesh,
        in_specs=placed,
        out_specs=P("tm", "space", None, None, None),
        check_vma=False,
    )
```

```python
import functools

import jax
import jax.numpy as jnp
from jax import lax
from jax.experimental import pallas as pl
from jax.experimental.pallas import tpu as pltpu
from jax.sharding import PartitionSpec as P

GROUPS = 32
ACROSS = 4
F32, BF16 = jnp.float32, jnp.bfloat16
SMALL = pltpu.CompilerParams(vmem_limit_bytes=8 << 20)
VMEM = pl.BlockSpec(memory_space=pltpu.VMEM)
AWAY = pl.BlockSpec(memory_space=pltpu.HBM)


def in_vmem(array):
    return pltpu.with_memory_space_constraint(array, pltpu.VMEM)


def in_hbm(array):
    return pltpu.with_memory_space_constraint(array, pltpu.HBM)


def cost(flops):
    return pl.CostEstimate(flops=flops, bytes_accessed=1 << 17, transcendentals=0)


def split(value):
    high = value.astype(BF16)
    rest = value - high.astype(F32)
    middle = rest.astype(BF16)
    low = (rest - middle.astype(F32)).astype(BF16)
    return high, middle, low


def exact_dot(value, table):
    parts = jnp.concatenate([part.astype(F32) for part in split(value)] + [jnp.zeros_like(value)], axis=0)
    product = jnp.dot(parts.astype(BF16), table.astype(BF16), preferred_element_type=F32)
    return product[0:8] + (product[8:16] + product[16:24])


def split_rows(row):
    place = lax.broadcasted_iota(jnp.int32, (16, 128), 0)
    block = jnp.zeros((16, 128), F32)
    for at, part in enumerate(split(row)):
        block = jnp.where(place == at, part.astype(F32), block)
    return block


def joined_row(block):
    return block[0:1] + block[1:2] + block[2:3]


def sums_kernel(frames_hbm, gain_hbm, shift_hbm, offset_hbm, message_ref, columns_ref, gain_ref, shift_ref,
                offset_ref, arrived, *, frames):
    rows, width, channels = frames_hbm.shape
    height = rows // frames
    per_group = channels // GROUPS
    part = rows // 4
    fetches = []
    for at in range(4):
        span = pl.ds(at * part, part)
        fetches.append(pltpu.make_async_copy(frames_hbm.at[span], message_ref.at[span], arrived.at[at]))
        fetches[-1].start()
    small = ((gain_hbm, gain_ref), (shift_hbm, shift_ref), (offset_hbm, offset_ref))
    for at, (source, target) in enumerate(small):
        fetches.append(pltpu.make_async_copy(source, target, arrived.at[4 + at]))
        fetches[-1].start()
    message_ref[rows:] = jnp.zeros((message_ref.shape[0] - rows, width, channels), BF16)
    kinds = 2 * frames
    source = lax.broadcasted_iota(jnp.int32, (kinds * channels, 128), 0)
    lane = lax.broadcasted_iota(jnp.int32, (kinds * channels, 128), 1)
    table = jnp.where(lane == source // per_group, 1.0, 0.0)
    plains, squares = [], []
    for frame in range(frames):
        plain = jnp.zeros((8, channels), F32)
        square = jnp.zeros((8, channels), F32)
        firsts, lasts = [], []
        for row in range(frame * height, (frame + 1) * height):
            if row % part == 0:
                fetches[row // part].wait()
            block = message_ref[row].astype(F32)
            firsts.append(block[0:1])
            lasts.append(block[width - 1 : width])
            block = block.reshape(width // 8, 8, channels)
            plain = plain + block.sum(0)
            square = square + (block * block).sum(0)
        plains.append(plain)
        squares.append(square)
        columns_ref[:, frame * channels : (frame + 1) * channels] = jnp.concatenate(firsts, axis=0).astype(BF16)
        at = (frames + frame) * channels
        columns_ref[:, at : at + channels] = jnp.concatenate(lasts, axis=0).astype(BF16)
    total = exact_dot(jnp.concatenate(plains + squares, axis=1), table)
    columns_ref[:, 2 * frames * channels :] = split_rows(total.sum(0, keepdims=True)).astype(BF16)
    for fetch in fetches[4:]:
        fetch.wait()


def group_sums(own, gain, shift, offset):
    count, height, width, channels = own.shape
    rows = count * height
    vector = jax.ShapeDtypeStruct(gain.shape, F32)
    return pl.pallas_call(
        functools.partial(sums_kernel, frames=count),
        out_shape=[
            jax.ShapeDtypeStruct((rows + 3 * count + 1, width, channels), BF16),
            jax.ShapeDtypeStruct((height, 2 * count * channels + 128), BF16),
            vector,
            vector,
            vector,
        ],
        in_specs=[AWAY] * 4,
        out_specs=[VMEM] * 5,
        scratch_shapes=[pltpu.SemaphoreType.DMA((7,))],
        compiler_params=SMALL,
        cost_estimate=cost(1 << 20),
    )(in_hbm(own.reshape(rows, width, channels)), in_hbm(gain), in_hbm(shift), in_hbm(offset))


def beside(index, step, count):
    return jnp.clip(index + step, 0, count - 1)


def rows_kernel(message_ref, sides_ref, taps_hbm, out_ref, *, frames, height):
    width, channels = message_ref.shape[1:]
    members, receivers = sides_ref.shape[0], out_ref.shape[0]
    tile = lax.axis_index("space")
    row_of, col_of = tile // ACROSS, tile % ACROSS
    on_left, on_right = beside(col_of, -1, members), beside(col_of, 1, members)
    ends_at = 2 * frames * channels
    total = jnp.zeros((1, 128), F32)
    for member in range(members):
        total = total + joined_row(sides_ref[member, :, ends_at : ends_at + 128].astype(F32))
    upper = lower = split_rows(total)
    place = lax.broadcasted_iota(jnp.int32, (16, 128), 0)
    for frame in range(frames):
        begin = (frames + frame) * channels
        left = sides_ref[on_left, :, begin : begin + channels].astype(F32)
        right = sides_ref[on_right, :, frame * channels : (frame + 1) * channels].astype(F32)
        for at, side in enumerate((left, right)):
            for half in range(2):
                row = place == 3 + 4 * frame + 2 * at + half
                lanes = slice(half * 128, (half + 1) * 128)
                upper = jnp.where(row, side[0:1, lanes], upper)
                lower = jnp.where(row, side[height - 1 : height, lanes], lower)
    for receiver in range(receivers):
        is_above = receiver < row_of
        for frame in range(frames):
            row = frame * height + jnp.where(is_above, 0, height - 1)
            for half in range(2):
                begin = (2 * frame + half) * channels
                out_ref[receiver, :, begin : begin + channels] = message_ref[row, half * 16 : half * 16 + 16]
        ends = jnp.where(is_above, upper, lower)
        out_ref[receiver, :, ends_at : ends_at + 128] = ends.astype(BF16)


def edge_rows(message, sides, taps, frames, height, receivers):
    width, channels = message.shape[1:]
    return pl.pallas_call(
        functools.partial(rows_kernel, frames=frames, height=height),
        out_shape=jax.ShapeDtypeStruct((receivers, width // 2, 2 * frames * channels + 128), BF16),
        in_specs=[VMEM, VMEM, AWAY],
        out_specs=VMEM,
        compiler_params=SMALL,
        cost_estimate=cost(1 << 20),
    )(message, sides, in_hbm(taps))


def border_kernel(message_ref, sides_ref, rows_ref, out_ref, sums_ref, *, frames, height):
    width, channels = message_ref.shape[1:]
    members, across = rows_ref.shape[0], sides_ref.shape[0]
    rows = frames * height
    tile = lax.axis_index("space")
    row_of, col_of = tile // ACROSS, tile % ACROSS
    on_left, on_right = beside(col_of, -1, across), beside(col_of, 1, across)
    above, below = beside(row_of, -1, members), beside(row_of, 1, members)
    ends_at = 2 * frames * channels
    total = jnp.zeros((1, 128), F32)
    for member in range(members):
        total = total + joined_row(rows_ref[member, :, ends_at : ends_at + 128].astype(F32))
    sums_ref[...] = jnp.broadcast_to(total[None], sums_ref.shape)
    upper = rows_ref[above, :, ends_at : ends_at + 128].astype(F32)
    lower = rows_ref[below, :, ends_at : ends_at + 128].astype(F32)
    place = lax.broadcasted_iota(jnp.int32, (16, channels), 0)
    corners = jnp.zeros((16, channels), F32)
    for frame in range(frames):
        at = rows + 3 * frame
        out_ref[at, 0:height] = sides_ref[on_left, :, (frames + frame) * channels : (frames + frame + 1) * channels]
        out_ref[at, height : 2 * height] = sides_ref[on_right, :, frame * channels : (frame + 1) * channels]
        for half in range(2):
            begin = (2 * frame + half) * channels
            out_ref[at + 1, half * 16 : half * 16 + 16] = rows_ref[above, :, begin : begin + channels]
            out_ref[at + 2, half * 16 : half * 16 + 16] = rows_ref[below, :, begin : begin + channels]
        cells = []
        for base in (3 + 4 * frame, 5 + 4 * frame):
            for block in (upper, lower):
                cells.append(jnp.concatenate([block[base : base + 1], block[base + 1 : base + 2]], axis=1))
        for index, cell in enumerate(cells):
            corners = jnp.where(place == 4 * frame + index, cell, corners)
    out_ref[rows + 3 * frames, 0:16] = corners.astype(BF16)


def add_border(message, sides, rows, frames, height, receivers):
    return pl.pallas_call(
        functools.partial(border_kernel, frames=frames, height=height),
        out_shape=[
            jax.ShapeDtypeStruct(message.shape, BF16),
            jax.ShapeDtypeStruct((receivers, 1, 128), F32),
        ],
        in_specs=[VMEM, VMEM, VMEM],
        out_specs=[VMEM, VMEM],
        input_output_aliases={0: 0},
        compiler_params=SMALL,
        cost_estimate=cost(1 << 20),
    )(message, sides, rows)


def norm_scales(sums, gain, time, cells):
    channels = gain.shape[1]
    per_group = channels // GROUPS
    index = lax.broadcasted_iota(jnp.int32, sums.shape, 0)
    lane = lax.broadcasted_iota(jnp.int32, (1, 128), 1)
    first = jnp.where((lane // GROUPS) % 2 == 0, 1.0, 0.0).astype(F32)
    before = jnp.where(index < time - 1, sums, 0.0).sum(0, keepdims=True)
    past = jnp.where(index == time - 1, sums, 0.0).sum(0, keepdims=True)
    own = jnp.where(index == time, sums, 0.0).sum(0, keepdims=True)
    running = jnp.concatenate(
        [before + past * first, before + past, before + past + own * first, before + past + own]
        + [jnp.zeros((4, 128), F32)],
        axis=0,
    )
    slot = lax.broadcasted_iota(jnp.int32, (128, 2 * channels), 0)
    target = lax.broadcasted_iota(jnp.int32, (128, 2 * channels), 1)
    table = (slot // (2 * GROUPS) == target // channels) & (slot % GROUPS == target % channels // per_group)
    wide = exact_dot(running, jnp.where(table, 1.0, 0.0))
    frame_row = lax.broadcasted_iota(jnp.int32, (8, channels), 0)
    count = jnp.maximum((time * 2 - 1 + frame_row) * cells, 1).astype(F32)
    mean = wide[:, :channels] / count
    spread = wide[:, channels:] / count - mean * mean
    return mean, lax.rsqrt(spread + 1e-06) * gain


def conv_kernel(sums_ref, past_ref, own_ref, gain_ref, shift_ref, offset_ref, taps_ref, out_hbm, shifted,
                out_ref, sent):
    frames, height, width, channels = out_ref.shape
    rows = frames * height
    time, tile, tiles = lax.axis_index("tm"), lax.axis_index("space"), lax.axis_size("space")
    row_of, col_of = tile // ACROSS, tile % ACROSS
    down_max = tiles // ACROSS - 1
    mean, scale = norm_scales(sums_ref[...], gain_ref[...], time, height * width * tiles * (channels // GROUPS))
    shift = shift_ref[...]

    def activate(value, which):
        u = (value.astype(F32) - mean[which : which + 1]) * scale[which : which + 1] + shift
        return u / (1.0 + jnp.exp(-u))

    has_left = jnp.where(col_of > 0, 1.0, 0.0).astype(F32)
    has_right = jnp.where(col_of < ACROSS - 1, 1.0, 0.0).astype(F32)
    has_up = jnp.where(row_of > 0, 1.0, 0.0).astype(F32)
    has_down = jnp.where(row_of < down_max, 1.0, 0.0).astype(F32)
    has_past = jnp.where(time > 0, 1.0, 0.0).astype(F32)
    place = lax.broadcasted_iota(jnp.int32, (width, channels), 0)

    def put(which, row, center, left, right):
        at = pl.ds((which * (height + 2) + row) * width, width)
        toward = jnp.where(place == 0, left, pltpu.roll(center, 1, 0))
        away = jnp.where(place == width - 1, right, pltpu.roll(center, width - 1, 0))
        shifted[at, 0:channels] = toward.astype(BF16)
        shifted[at, channels : 2 * channels] = center.astype(BF16)
        shifted[at, 2 * channels : 3 * channels] = away.astype(BF16)

    def prepare(which):
        source = past_ref if which < 2 else own_ref
        here = has_past if which < 2 else jnp.ones((), F32)
        frame = which % 2
        at = rows + 3 * frame
        left = activate(source[at, 0:height], which) * (has_left * here)
        right = activate(source[at, height : 2 * height], which) * (has_right * here)
        up = activate(source[at + 1], which) * (has_up * here)
        down = activate(source[at + 2], which) * (has_down * here)
        corners = activate(source[rows + 3 * frames, 0:16], which) * here
        corners = corners[4 * frame : 4 * frame + 4]
        put(which, 0, up, corners[0:1] * (has_up * has_left), corners[2:3] * (has_up * has_right))
        put(which, height + 1, down, corners[1:2] * (has_down * has_left), corners[3:4] * (has_down * has_right))
        for row in range(height):
            center = activate(source[frame * height + row], which)
            if which < 2:
                center = center * here
            put(which, row + 1, center, left[row : row + 1], right[row : row + 1])

    pieces = 4
    size = height * width // pieces
    totals = {}
    sends = []

    def gather(which):
        for frame in range(frames):
            lagged = which - frame
            if not 0 <= lagged < 3:
                continue
            for piece in range(pieces):
                for vertical in range(3):
                    at = (which * (height + 2) + vertical) * width + piece * size
                    part = jnp.dot(
                        shifted[at : at + size, :], taps_ref[lagged * 3 + vertical], preferred_element_type=F32
                    )
                    totals[frame, piece] = totals[frame, piece] + part if (frame, piece) in totals else part
                if lagged == 2:
                    finish(frame, piece)

    def finish(frame, piece):
        span = height // pieces
        value = own_ref[frame * height + piece * span : frame * height + (piece + 1) * span]
        value = value.astype(F32).reshape(size, channels) + (totals[frame, piece] + offset_ref[...])
        rows = pl.ds(piece * span, span)
        out_ref[frame, rows] = value.astype(BF16).reshape(span, width, channels)
        sends.append(pltpu.make_async_copy(
            out_ref.at[frame, rows], out_hbm.at[frame, rows], sent.at[frame * pieces + piece]))
        sends[-1].start()

    for which in range(4):
        prepare(which)
        gather(which)
    for send in sends:
        send.wait()


def convolve(sums, past, own, gain, shift, offset, taps, shape):
    frames, height, width, channels = shape
    return pl.pallas_call(
        conv_kernel,
        out_shape=pltpu.HBM(shape, BF16),
        in_specs=[VMEM] * 7,
        out_specs=AWAY,
        scratch_shapes=[
            pltpu.VMEM((4 * (height + 2) * width, 3 * channels), BF16),
            pltpu.VMEM(shape, BF16),
            pltpu.SemaphoreType.DMA((4 * frames,)),
        ],
        compiler_params=pltpu.CompilerParams(vmem_limit_bytes=32 << 20),
        cost_estimate=pl.CostEstimate(flops=4 << 30, bytes_accessed=6 << 20, transcendentals=1 << 20),
    )(sums, past, own, gain, shift, offset, in_vmem(taps))


def local(frames, norm_gain, norm_shift, conv_filter, conv_offset):
    own = frames[:, 0]
    count, height, width, channels = own.shape
    times, tiles = lax.axis_size("tm"), lax.axis_size("space")

    later = [(t, t + 1) for t in range(times - 1)]
    across = [[row + col for col in range(ACROSS)] for row in range(0, tiles, ACROSS)]
    along = [[row + col for row in range(0, tiles, ACROSS)] for col in range(ACROSS)]

    message, columns, gain, shift, offset = group_sums(own, norm_gain[None], norm_shift[None], conv_offset[None])
    sides = lax.all_gather(columns, "space", axis_index_groups=across)
    taps = conv_filter.reshape(9, 3 * channels, channels)
    rows = edge_rows(message, sides, taps, count, height, tiles // ACROSS)
    rows = lax.all_to_all(rows, "space", 0, 0, axis_index_groups=along)
    message, sums = add_border(message, sides, rows, count, height, times)
    past = lax.ppermute(message, "tm", later)
    sums = lax.all_to_all(sums, "tm", 0, 0).reshape(times, 128)

    taps = conv_filter.reshape(9, 3 * channels, channels)
    output = convolve(sums, past, message, gain, shift, offset, taps, own.shape)
    return output[:, None]


def solution(mesh):
    placed = (P("tm", "space", None, None, None), P(), P(), P(), P())
    return jax.shard_map(
        local,
        mesh=mesh,
        in_specs=placed,
        out_specs=P("tm", "space", None, None, None),
        check_vma=False,
    )
```

```python
import functools

import jax
import jax.numpy as jnp
from jax import lax
from jax.experimental import pallas as pl
from jax.experimental.pallas import tpu as pltpu
from jax.sharding import PartitionSpec as P

GROUPS = 32
ACROSS = 4
F32, BF16 = jnp.float32, jnp.bfloat16
SMALL = pltpu.CompilerParams(vmem_limit_bytes=8 << 20)
VMEM = pl.BlockSpec(memory_space=pltpu.VMEM)
AWAY = pl.BlockSpec(memory_space=pltpu.HBM)


def in_vmem(array):
    return pltpu.with_memory_space_constraint(array, pltpu.VMEM)


def in_hbm(array):
    return pltpu.with_memory_space_constraint(array, pltpu.HBM)


def cost(flops):
    return pl.CostEstimate(flops=flops, bytes_accessed=1 << 17, transcendentals=0)


def split(value):
    high = value.astype(BF16)
    rest = value - high.astype(F32)
    middle = rest.astype(BF16)
    low = (rest - middle.astype(F32)).astype(BF16)
    return high, middle, low


def exact_dot(value, table):
    parts = jnp.concatenate([part.astype(F32) for part in split(value)] + [jnp.zeros_like(value)], axis=0)
    product = jnp.dot(parts.astype(BF16), table.astype(BF16), preferred_element_type=F32)
    return product[0:8] + (product[8:16] + product[16:24])


def split_rows(row):
    place = lax.broadcasted_iota(jnp.int32, (16, 128), 0)
    block = jnp.zeros((16, 128), F32)
    for at, part in enumerate(split(row)):
        block = jnp.where(place == at, part.astype(F32), block)
    return block


def joined_row(block):
    return block[0:1] + block[1:2] + block[2:3]


def sums_kernel(frames_hbm, gain_hbm, shift_hbm, offset_hbm, message_ref, columns_ref, gain_ref, shift_ref,
                offset_ref, arrived, *, frames):
    blocks, half, channels = frames_hbm.shape
    rows, width = blocks // 2, 2 * half
    height = rows // frames
    per_group = channels // GROUPS
    part = rows // 4
    fetches = []
    for at in range(4):
        span = pl.ds(at * 2 * part, 2 * part)
        fetches.append(pltpu.make_async_copy(frames_hbm.at[span], message_ref.at[span], arrived.at[at]))
        fetches[-1].start()
    small = ((gain_hbm, gain_ref), (shift_hbm, shift_ref), (offset_hbm, offset_ref))
    for at, (source, target) in enumerate(small):
        fetches.append(pltpu.make_async_copy(source, target, arrived.at[4 + at]))
        fetches[-1].start()
    message_ref[blocks:] = jnp.zeros((message_ref.shape[0] - blocks, half, channels), BF16)
    kinds = 2 * frames
    source = lax.broadcasted_iota(jnp.int32, (kinds * channels, 128), 0)
    lane = lax.broadcasted_iota(jnp.int32, (kinds * channels, 128), 1)
    table = jnp.where(lane == source // per_group, 1.0, 0.0)
    plains, squares = [], []
    for frame in range(frames):
        plain = jnp.zeros((8, channels), F32)
        square = jnp.zeros((8, channels), F32)
        firsts, lasts = [], []
        for row in range(frame * height, (frame + 1) * height):
            if row % part == 0:
                fetches[row // part].wait()
            block = message_ref[2 * row : 2 * row + 2].astype(F32).reshape(width, channels)
            firsts.append(block[0:1])
            lasts.append(block[width - 1 : width])
            block = block.reshape(width // 8, 8, channels)
            plain = plain + block.sum(0)
            square = square + (block * block).sum(0)
        plains.append(plain)
        squares.append(square)
        columns_ref[:, frame * channels : (frame + 1) * channels] = jnp.concatenate(firsts, axis=0).astype(BF16)
        at = (frames + frame) * channels
        columns_ref[:, at : at + channels] = jnp.concatenate(lasts, axis=0).astype(BF16)
    total = exact_dot(jnp.concatenate(plains + squares, axis=1), table)
    columns_ref[:, 2 * frames * channels :] = split_rows(total.sum(0, keepdims=True)).astype(BF16)
    for fetch in fetches[4:]:
        fetch.wait()


def group_sums(own, gain, shift, offset):
    count, height, width, channels = own.shape
    rows = count * height
    vector = jax.ShapeDtypeStruct(gain.shape, F32)
    return pl.pallas_call(
        functools.partial(sums_kernel, frames=count),
        out_shape=[
            jax.ShapeDtypeStruct((2 * rows + 6 * count + 1, width // 2, channels), BF16),
            jax.ShapeDtypeStruct((height, 2 * count * channels + 128), BF16),
            vector,
            vector,
            vector,
        ],
        in_specs=[AWAY] * 4,
        out_specs=[VMEM] * 5,
        scratch_shapes=[pltpu.SemaphoreType.DMA((7,))],
        compiler_params=SMALL,
        cost_estimate=cost(1 << 20),
    )(in_hbm(own.reshape(2 * rows, width // 2, channels)), in_hbm(gain), in_hbm(shift), in_hbm(offset))


def beside(index, step, count):
    return jnp.clip(index + step, 0, count - 1)


def rows_kernel(message_ref, sides_ref, taps_hbm, out_ref, *, frames, height):
    channels = message_ref.shape[2]
    members, receivers = sides_ref.shape[0], out_ref.shape[0]
    tile = lax.axis_index("space")
    row_of, col_of = tile // ACROSS, tile % ACROSS
    on_left, on_right = beside(col_of, -1, members), beside(col_of, 1, members)
    ends_at = 2 * frames * channels
    total = jnp.zeros((1, 128), F32)
    for member in range(members):
        total = total + joined_row(sides_ref[member, :, ends_at : ends_at + 128].astype(F32))
    upper = lower = split_rows(total)
    place = lax.broadcasted_iota(jnp.int32, (16, 128), 0)
    for frame in range(frames):
        begin = (frames + frame) * channels
        left = sides_ref[on_left, :, begin : begin + channels].astype(F32)
        right = sides_ref[on_right, :, frame * channels : (frame + 1) * channels].astype(F32)
        for at, side in enumerate((left, right)):
            for half in range(2):
                row = place == 3 + 4 * frame + 2 * at + half
                lanes = slice(half * 128, (half + 1) * 128)
                upper = jnp.where(row, side[0:1, lanes], upper)
                lower = jnp.where(row, side[height - 1 : height, lanes], lower)
    for receiver in range(receivers):
        is_above = receiver < row_of
        for frame in range(frames):
            row = frame * height + jnp.where(is_above, 0, height - 1)
            for half in range(2):
                begin = (2 * frame + half) * channels
                out_ref[receiver, :, begin : begin + channels] = message_ref[2 * row + half]
        ends = jnp.where(is_above, upper, lower)
        out_ref[receiver, :, ends_at : ends_at + 128] = ends.astype(BF16)


def edge_rows(message, sides, taps, frames, height, receivers):
    width, channels = 2 * message.shape[1], message.shape[2]
    return pl.pallas_call(
        functools.partial(rows_kernel, frames=frames, height=height),
        out_shape=jax.ShapeDtypeStruct((receivers, width // 2, 2 * frames * channels + 128), BF16),
        in_specs=[VMEM, VMEM, AWAY],
        out_specs=VMEM,
        compiler_params=SMALL,
        cost_estimate=cost(1 << 20),
    )(message, sides, in_hbm(taps))


def border_kernel(message_ref, sides_ref, rows_ref, out_ref, sums_ref, *, frames, height):
    channels = message_ref.shape[2]
    members, across = rows_ref.shape[0], sides_ref.shape[0]
    rows = frames * height
    tile = lax.axis_index("space")
    row_of, col_of = tile // ACROSS, tile % ACROSS
    on_left, on_right = beside(col_of, -1, across), beside(col_of, 1, across)
    above, below = beside(row_of, -1, members), beside(row_of, 1, members)
    ends_at = 2 * frames * channels
    total = jnp.zeros((1, 128), F32)
    for member in range(members):
        total = total + joined_row(rows_ref[member, :, ends_at : ends_at + 128].astype(F32))
    sums_ref[...] = jnp.broadcast_to(total[None], sums_ref.shape)
    upper = rows_ref[above, :, ends_at : ends_at + 128].astype(F32)
    lower = rows_ref[below, :, ends_at : ends_at + 128].astype(F32)
    place = lax.broadcasted_iota(jnp.int32, (16, channels), 0)
    corners = jnp.zeros((16, channels), F32)
    for frame in range(frames):
        at = 2 * rows + 6 * frame
        out_ref[at] = sides_ref[on_left, :, (frames + frame) * channels : (frames + frame + 1) * channels]
        out_ref[at + 1] = sides_ref[on_right, :, frame * channels : (frame + 1) * channels]
        for half in range(2):
            begin = (2 * frame + half) * channels
            out_ref[at + 2 + half] = rows_ref[above, :, begin : begin + channels]
            out_ref[at + 4 + half] = rows_ref[below, :, begin : begin + channels]
        cells = []
        for base in (3 + 4 * frame, 5 + 4 * frame):
            for block in (upper, lower):
                cells.append(jnp.concatenate([block[base : base + 1], block[base + 1 : base + 2]], axis=1))
        for index, cell in enumerate(cells):
            corners = jnp.where(place == 4 * frame + index, cell, corners)
    out_ref[2 * rows + 6 * frames] = corners.astype(BF16)


def add_border(message, sides, rows, frames, height, receivers):
    return pl.pallas_call(
        functools.partial(border_kernel, frames=frames, height=height),
        out_shape=[
            jax.ShapeDtypeStruct(message.shape, BF16),
            jax.ShapeDtypeStruct((receivers, 1, 128), F32),
        ],
        in_specs=[VMEM, VMEM, VMEM],
        out_specs=[VMEM, VMEM],
        input_output_aliases={0: 0},
        compiler_params=SMALL,
        cost_estimate=cost(1 << 20),
    )(message, sides, rows)


def norm_scales(sums, gain, time, cells):
    channels = gain.shape[1]
    per_group = channels // GROUPS
    index = lax.broadcasted_iota(jnp.int32, sums.shape, 0)
    lane = lax.broadcasted_iota(jnp.int32, (1, 128), 1)
    first = jnp.where((lane // GROUPS) % 2 == 0, 1.0, 0.0).astype(F32)
    before = jnp.where(index < time - 1, sums, 0.0).sum(0, keepdims=True)
    past = jnp.where(index == time - 1, sums, 0.0).sum(0, keepdims=True)
    own = jnp.where(index == time, sums, 0.0).sum(0, keepdims=True)
    running = jnp.concatenate(
        [before + past * first, before + past, before + past + own * first, before + past + own]
        + [jnp.zeros((4, 128), F32)],
        axis=0,
    )
    slot = lax.broadcasted_iota(jnp.int32, (128, 2 * channels), 0)
    target = lax.broadcasted_iota(jnp.int32, (128, 2 * channels), 1)
    table = (slot // (2 * GROUPS) == target // channels) & (slot % GROUPS == target % channels // per_group)
    wide = exact_dot(running, jnp.where(table, 1.0, 0.0))
    frame_row = lax.broadcasted_iota(jnp.int32, (8, channels), 0)
    count = jnp.maximum((time * 2 - 1 + frame_row) * cells, 1).astype(F32)
    mean = wide[:, :channels] / count
    spread = wide[:, channels:] / count - mean * mean
    return mean, lax.rsqrt(spread + 1e-06) * gain


def conv_kernel(sums_ref, past_ref, own_ref, gain_ref, shift_ref, offset_ref, taps_ref, out_hbm, shifted,
                out_ref, sent):
    frames, height, width, channels = out_ref.shape
    rows = frames * height
    time, tile, tiles = lax.axis_index("tm"), lax.axis_index("space"), lax.axis_size("space")
    row_of, col_of = tile // ACROSS, tile % ACROSS
    down_max = tiles // ACROSS - 1
    mean, scale = norm_scales(sums_ref[...], gain_ref[...], time, height * width * tiles * (channels // GROUPS))
    shift = shift_ref[...]

    def activate(value, which):
        u = (value.astype(F32) - mean[which : which + 1]) * scale[which : which + 1] + shift
        return u / (1.0 + jnp.exp(-u))

    has_left = jnp.where(col_of > 0, 1.0, 0.0).astype(F32)
    has_right = jnp.where(col_of < ACROSS - 1, 1.0, 0.0).astype(F32)
    has_up = jnp.where(row_of > 0, 1.0, 0.0).astype(F32)
    has_down = jnp.where(row_of < down_max, 1.0, 0.0).astype(F32)
    has_past = jnp.where(time > 0, 1.0, 0.0).astype(F32)
    place = lax.broadcasted_iota(jnp.int32, (width, channels), 0)

    def put(which, row, center, left, right):
        at = pl.ds((which * (height + 2) + row) * width, width)
        toward = jnp.where(place == 0, left, pltpu.roll(center, 1, 0))
        away = jnp.where(place == width - 1, right, pltpu.roll(center, width - 1, 0))
        shifted[at, 0:channels] = toward.astype(BF16)
        shifted[at, channels : 2 * channels] = center.astype(BF16)
        shifted[at, 2 * channels : 3 * channels] = away.astype(BF16)

    def prepare(which):
        source = past_ref if which < 2 else own_ref
        here = has_past if which < 2 else jnp.ones((), F32)
        frame = which % 2
        at = 2 * rows + 6 * frame
        left = activate(source[at], which) * (has_left * here)
        right = activate(source[at + 1], which) * (has_right * here)
        up = activate(source[at + 2 : at + 4].reshape(width, channels), which) * (has_up * here)
        down = activate(source[at + 4 : at + 6].reshape(width, channels), which) * (has_down * here)
        corners = activate(source[2 * rows + 6 * frames], which) * here
        corners = corners[4 * frame : 4 * frame + 4]
        put(which, 0, up, corners[0:1] * (has_up * has_left), corners[2:3] * (has_up * has_right))
        put(which, height + 1, down, corners[1:2] * (has_down * has_left), corners[3:4] * (has_down * has_right))
        for row in range(height):
            begin = 2 * (frame * height + row)
            center = activate(source[begin : begin + 2].reshape(width, channels), which)
            if which < 2:
                center = center * here
            put(which, row + 1, center, left[row : row + 1], right[row : row + 1])

    pieces = 4
    size = height * width // pieces
    totals = {}
    sends = []

    def gather(which):
        for frame in range(frames):
            lagged = which - frame
            if not 0 <= lagged < 3:
                continue
            for piece in range(pieces):
                for vertical in range(3):
                    at = (which * (height + 2) + vertical) * width + piece * size
                    part = jnp.dot(
                        shifted[at : at + size, :], taps_ref[lagged * 3 + vertical], preferred_element_type=F32
                    )
                    totals[frame, piece] = totals[frame, piece] + part if (frame, piece) in totals else part
                if lagged == 2:
                    finish(frame, piece)

    def finish(frame, piece):
        span = height // pieces
        begin = 2 * (frame * height + piece * span)
        value = own_ref[begin : begin + 2 * span]
        value = value.astype(F32).reshape(size, channels) + (totals[frame, piece] + offset_ref[...])
        rows = pl.ds(piece * span, span)
        out_ref[frame, rows] = value.astype(BF16).reshape(span, width, channels)
        sends.append(pltpu.make_async_copy(
            out_ref.at[frame, rows], out_hbm.at[frame, rows], sent.at[frame * pieces + piece]))
        sends[-1].start()

    for which in range(4):
        prepare(which)
        gather(which)
    for send in sends:
        send.wait()


def convolve(sums, past, own, gain, shift, offset, taps, shape):
    frames, height, width, channels = shape
    return pl.pallas_call(
        conv_kernel,
        out_shape=pltpu.HBM(shape, BF16),
        in_specs=[VMEM] * 7,
        out_specs=AWAY,
        scratch_shapes=[
            pltpu.VMEM((4 * (height + 2) * width, 3 * channels), BF16),
            pltpu.VMEM(shape, BF16),
            pltpu.SemaphoreType.DMA((4 * frames,)),
        ],
        compiler_params=pltpu.CompilerParams(vmem_limit_bytes=32 << 20),
        cost_estimate=pl.CostEstimate(flops=4 << 30, bytes_accessed=6 << 20, transcendentals=1 << 20),
    )(sums, past, own, gain, shift, offset, in_vmem(taps))


def local(frames, norm_gain, norm_shift, conv_filter, conv_offset):
    own = frames[:, 0]
    count, height, width, channels = own.shape
    times, tiles = lax.axis_size("tm"), lax.axis_size("space")

    later = [(t, t + 1) for t in range(times - 1)]
    across = [[row + col for col in range(ACROSS)] for row in range(0, tiles, ACROSS)]
    along = [[row + col for row in range(0, tiles, ACROSS)] for col in range(ACROSS)]

    message, columns, gain, shift, offset = group_sums(own, norm_gain[None], norm_shift[None], conv_offset[None])
    sides = lax.all_gather(columns, "space", axis_index_groups=across)
    taps = conv_filter.reshape(9, 3 * channels, channels)
    rows = edge_rows(message, sides, taps, count, height, tiles // ACROSS)
    rows = lax.all_to_all(rows, "space", 0, 0, axis_index_groups=along)
    message, sums = add_border(message, sides, rows, count, height, times)
    past = lax.ppermute(message, "tm", later)
    sums = lax.all_to_all(sums, "tm", 0, 0).reshape(times, 128)

    taps = conv_filter.reshape(9, 3 * channels, channels)
    output = convolve(sums, past, message, gain, shift, offset, taps, own.shape)
    return output[:, None]


def solution(mesh):
    placed = (P("tm", "space", None, None, None), P(), P(), P(), P())
    return jax.shard_map(
        local,
        mesh=mesh,
        in_specs=placed,
        out_specs=P("tm", "space", None, None, None),
        check_vma=False,
    )
```
